32 devices in a mesh: section: 2 (over y), dp: 4 (over x, core), cell: 4 (over z).
Axes of the slice: x: 2, y: 2, z: 4, core: 2. Of those that a mesh axis runs over, the one named last changes fastest.
Arguments:
- probes: float32 [2, 3072, 128], P('section', 'cell'), may hold values from -6 to 6
- jacobian: float32 [2, 4096, 3072], P('section', 'dp', 'cell'), may hold values from -0.109375 to 0.109375
- classes: int32 [2, 4096], P('section', 'dp'), may hold values from 0 to 3
- active: int32 [2, 3072], P('section', 'cell'), may hold values 0 or 1
- coupling: float32 [2, 3072], P('section', 'cell'), may hold values from 0.1 to 1
Outputs:
- first_image: float32 [2, 3072, 128], P('section', 'cell')
- second_image: float32 [2, 3072, 128], P('section', 'cell')
The draws below stay inside these ranges and needn't reach their ends.
All inputs are finite; a program needn't handle non-finite values. No bound on the sum of `active` on one device may be relied on, other than what follows from the above.
Results may differ from the reference program's by a relative error of at most 0.000092.
Values sent between devices are 32-bit elements; how exact they have to be, the bound alone decides.
No kernel may reach another device: no remote copies, remote signals or barrier semaphores. Data moves between devices by JAX's collectives and lax.ppermute only.
A program may use at most 64 MiB of HBM per device.

```python
import math
import jax
import jax.numpy as jnp
from jax import lax

PROBES = 128
SECTIONS = 2
NDATA = 4096
NCELL = 3072


def touch_ends(drawn, rng, smallest, top_value):
    longest = drawn.shape.index(max(drawn.shape))
    spots = []
    for shift in (0, 1):
        where = [jax.random.randint(jax.random.fold_in(rng, axis), (), 0, length) for axis, length in enumerate(drawn.shape)]
        where[longest] = (where[longest] + shift) % drawn.shape[longest]
        spots.append(tuple(where))
    return drawn.at[spots[0]].set(smallest).at[spots[1]].set(top_value)


def block_levels(stream_key, dims, pieces, least, high):
    level, own = 1.0, jax.random.fold_in(stream_key, 6)
    for dim, blocks in pieces:
        steps = jnp.exp(jax.random.uniform(jax.random.fold_in(own, dim), (blocks,), jnp.float32, least / len(pieces), high / len(pieces)))
        level = level * jnp.repeat(steps, dims[dim] // blocks).reshape([-1 if axis == dim else 1 for axis in range(len(dims))])
    return level


def gaussian(stream_key, extent, width, reach, cuts=(), held_as=jnp.bfloat16):
    level = block_levels(stream_key, extent, cuts, -0.22, 0.18) if cuts else 1.0
    result = jax.random.normal(stream_key, extent, jnp.float32) * width * level
    return jnp.minimum(jnp.maximum(result, -reach), reach).astype(held_as)


def setup_inputs(seed: int = 0) -> dict:
    seeds = jax.random.split(jax.random.key(seed), 6)
    probes = gaussian(seeds[0], (SECTIONS, NCELL, PROBES), 1.0, 6.0, ((0, 2), (1, 4)), jnp.float32)
    jacobian = gaussian(seeds[1], (SECTIONS, NDATA, NCELL), NCELL ** -0.5, 0.109375, ((0, 2), (1, 4), (2, 4)), jnp.float32)
    classes = touch_ends(jax.random.randint(seeds[2], (SECTIONS, NDATA), 0, 4), jax.random.fold_in(seeds[2], 1), 0, 3).astype(jnp.int32)
    active = touch_ends((jax.random.randint(seeds[3], (SECTIONS, NCELL), 0, 4) < 3).astype(jnp.int32), jax.random.fold_in(seeds[3], 1), 0, 1)
    coupling = jnp.clip(jnp.exp(math.log(1.0) - 2.3025851 * jax.random.uniform(seeds[4], (SECTIONS, NCELL), jnp.float32) ** block_levels(seeds[4], (SECTIONS, NCELL), ((0, 2), (1, 4)), -0.2, 0.2)), 0.1, 1.0)
    return dict(probes=probes, jacobian=jacobian, classes=classes, active=active, coupling=coupling)


def section_product(items):
    tile, field, factor = items
    forward = jnp.dot(tile, field, precision=lax.Precision.HIGHEST, preferred_element_type=jnp.float32)
    weighted = forward * factor[:, None]
    return lax.dot_general(tile, weighted, (((0,), (0,)), ((), ())), precision=lax.Precision.HIGHEST, preferred_element_type=jnp.float32)


def apply_hessian(field, jacobian, factors, maskf, strength, strength_next):
    masked = field * maskf[:, :, None]
    back = lax.map(section_product, (jacobian, masked, factors))
    zero_row = jnp.zeros_like(masked[:1])
    below = jnp.concatenate([zero_row, masked[:-1]], axis=0)
    above = jnp.concatenate([masked[1:], zero_row], axis=0)
    smooth = strength[:, :, None] * (masked - below) + strength_next[:, :, None] * (masked - above)
    return maskf[:, :, None] * (back + smooth)


def reference(probes, jacobian, classes, active, coupling):
    table = jnp.array([1.0, 0.5, 0.25, 0.125], dtype=jnp.float32)
    factors = table[classes]
    maskf = active.astype(jnp.float32)
    strength = coupling.at[0].set(0.0)
    strength_next = jnp.concatenate([strength[1:], jnp.zeros_like(strength[:1])], axis=0)
    first_image = apply_hessian(probes, jacobian, factors, maskf, strength, strength_next)
    second_image = apply_hessian(first_image, jacobian, factors, maskf, strength, strength_next)
    return first_image, second_image
```

```python
import jax
import jax.numpy as jnp
from jax import lax
from jax.sharding import PartitionSpec as P

CHUNKS = 1


def xor_pairs(axis, stride):
    return [(i, i ^ stride) for i in range(lax.axis_size(axis))]


def swap(value, axis, stride):
    return lax.ppermute(value, axis, xor_pairs(axis, stride))


def shifted(value, axis, by):
    length = lax.axis_size(axis)
    pairs = [(i, i + by) for i in range(length) if 0 <= i + by < length]
    return lax.ppermute(value, axis, pairs)


def class_weight(labels):
    return jnp.where(
        labels == 0, 1.0, jnp.where(labels == 1, 0.5, jnp.where(labels == 2, 0.25, 0.125))
    ).astype(jnp.float32)


def local(probes, jacobian, classes, active, coupling):
    tile = jacobian[0]
    factors = class_weight(classes[0])[None, :]
    cells = tile.shape[1]
    half = cells // 2
    cell_parts = lax.axis_size("cell")
    dp_parts = lax.axis_size("dp")
    here = lax.axis_index("cell")
    side = lax.axis_index("dp") % 2
    first_section = lax.axis_index("section") == 0

    def own_first(value, axis):
        size = value.shape[axis] // 2
        return jnp.concatenate(
            [
                lax.dynamic_slice_in_dim(value, side * size, size, axis),
                lax.dynamic_slice_in_dim(value, (1 - side) * size, size, axis),
            ],
            axis=axis,
        )

    def reorder(value):
        size = value.shape[0] // cell_parts
        return jnp.concatenate(
            [
                lax.dynamic_slice_in_dim(value, (here ^ x) * size, size, 0)
                for x in range(cell_parts)
            ],
            axis=0,
        )

    tile = own_first(tile, 1)
    maskf = own_first(active[0].astype(jnp.float32), 0)[None, :]
    strength = jnp.where(first_section, 0.0, own_first(coupling[0], 0)[None, :half])
    strength_next = shifted(strength, "section", -1)

    def forward(masked):
        return lax.dot_general(
            masked,
            tile,
            (((1,), (1,)), ((), ())),
            precision=lax.Precision.HIGH,
            preferred_element_type=jnp.float32,
        )

    def backward(weighted):
        return jnp.dot(
            weighted, tile, precision=lax.Precision.HIGH, preferred_element_type=jnp.float32
        )

    def sum_cells(part):
        size = part.shape[0] // cell_parts
        total = part[:size]
        for x in range(cell_parts - 1, 0, -1):
            total = total + swap(part[x * size : (x + 1) * size], "cell", x)
        total = total * factors
        blocks = [total] + [swap(total, "cell", x) for x in range(1, cell_parts)]
        return jnp.concatenate(blocks, axis=0)

    def sum_data(part):
        total = part[:, :half] + swap(part[:, half:], "dp", 1)
        stride = 2
        while stride < dp_parts:
            total = total + swap(total, "dp", stride)
            stride *= 2
        return total

    def smoothing(masked):
        below = shifted(masked, "section", 1)
        above = shifted(masked, "section", -1)
        return strength * (masked - below) + strength_next * (masked - above)

    def apply_hessian(field):
        masked = field * maskf
        smooth = smoothing(masked[:, :half])
        back = sum_data(backward(sum_cells(forward(masked))))
        image = maskf[:, :half] * (back + smooth)
        return jnp.concatenate([image, swap(image, "dp", 1)], axis=1)

    def chunked(function, value):
        size = value.shape[0] // CHUNKS
        return [function(value[i * size : (i + 1) * size]) for i in range(CHUNKS)]

    def finish(parts):
        rows = jnp.concatenate([reorder(part) for part in parts], axis=0)
        return own_first(rows, 1).T[None]

    start = probes[0].T
    start = own_first(start, 1)
    first = chunked(lambda part: apply_hessian(reorder(part)), start)
    second = [apply_hessian(part) for part in first]
    return finish(first), finish(second)


def solution(mesh):
    return jax.shard_map(
        local,
        mesh=mesh,
        in_specs=(
            P("section", "cell", None),
            P("section", "dp", "cell"),
            P("section", "dp"),
            P("section", "cell"),
            P("section", "cell"),
        ),
        out_specs=(P("section", "cell", None), P("section", "cell", None)),
        check_vma=False,
    )
```

```python
import functools

import jax
import jax.numpy as jnp
from jax import lax
from jax.experimental import pallas as pl
from jax.experimental.pallas import tpu as pltpu
from jax.sharding import PartitionSpec as P

MAX_CHUNKS = 1
LIMIT = 24 * 2**20
NT = (((1,), (1,)), ((), ()))
NN = (((1,), (0,)), ((), ()))
VMEM = pl.BlockSpec(memory_space=pltpu.VMEM)


def swap(value, axis, stride):
    return lax.ppermute(value, axis, [(i, i ^ stride) for i in range(lax.axis_size(axis))])


def shifted(value, axis, by):
    length = lax.axis_size(axis)
    pairs = [(i, i + by) for i in range(length) if 0 <= i + by < length]
    return lax.ppermute(value, axis, pairs)


def split(value):
    high = value.astype(jnp.bfloat16)
    return high, (value - high.astype(jnp.float32)).astype(jnp.bfloat16)


def product(value, high, low, dims):
    top, rest = split(value)
    rows = value.shape[0]
    dot = functools.partial(
        lax.dot_general, dimension_numbers=dims, preferred_element_type=jnp.float32
    )
    both = dot(jnp.concatenate([top, rest], axis=0), high)
    return both[:rows] + (both[rows:] + dot(top, low))


def call(kernel, shapes, operands, flops=0):
    return pl.pallas_call(
        kernel,
        out_shape=shapes,
        in_specs=[VMEM] * len(operands),
        out_specs=[VMEM] * len(shapes),
        compiler_params=pltpu.CompilerParams(vmem_limit_bytes=LIMIT),
        cost_estimate=pl.CostEstimate(
            flops=flops, bytes_accessed=sum(4 * o.size for o in operands), transcendentals=0
        ),
    )(*operands)


def own_first(ref, rows, side, half):
    own = pl.ds(pl.multiple_of(side * half, half), half)
    other = pl.ds(pl.multiple_of((1 - side) * half, half), half)
    return jnp.concatenate([ref[rows, own], ref[rows, other]], axis=1)


def first_kernel(chunks, parts, *refs):
    probes, tile, classes, active, coupling, high, low, mask, weight, message = refs[:10]
    blocks = refs[10:-2]
    turned, masked = refs[-2:]
    side = lax.axis_index("dp") % 2
    here = lax.axis_index("cell")
    cells, count = probes.shape
    half = cells // 2
    size = count // (chunks * parts)
    every = slice(None)

    @pl.when(pl.program_id(0) == 0)
    def _():
        keep = own_first(active, every, side, half).astype(jnp.float32)
        mask[...] = keep
        turned[...] = probes[...].T
        for chunk in range(chunks):
            for x in range(parts):
                spot = (chunk * parts + x) * size
                start = pl.multiple_of((chunk * parts + (here ^ x)) * size, size)
                masked[spot : spot + size, :] = (
                    own_first(turned, pl.ds(start, size), side, half) * keep
                )
        message[:count, :] = masked[:, :half]
        own = own_first(coupling, every, side, half)[:, :half]
        message[count:, :] = jnp.broadcast_to(own, (8, half))
        labels = classes[...]
        weight[...] = jnp.where(
            labels == 0, 1.0, jnp.where(labels == 1, 0.5, jnp.where(labels == 2, 0.25, 0.125))
        ).astype(jnp.float32)

    top, rest = split(own_first(tile, every, side, half))
    high[...] = top
    low[...] = rest
    out = product(masked[...], top, rest, NT)
    for index, block in enumerate(blocks):
        block[...] = out[index * size : (index + 1) * size]


def first_forward(probes, tile, classes, active, coupling, chunks):
    parts = lax.axis_size("cell")
    cells, count = probes.shape
    data = tile.shape[0]
    size = count // (chunks * parts)
    step = 256 if data % 256 == 0 else data
    whole = lambda shape: pl.BlockSpec(shape, lambda i: (0,) * len(shape))
    shape = jax.ShapeDtypeStruct
    rows = pl.BlockSpec((step, cells), lambda i: (i, 0))
    outs = pl.pallas_call(
        functools.partial(first_kernel, chunks, parts),
        grid=(data // step,),
        in_specs=[
            whole((cells, count)),
            rows,
            whole((1, data)),
            whole((1, cells)),
            whole((1, cells)),
        ],
        out_specs=[
            rows,
            rows,
            whole((1, cells)),
            whole((1, data)),
            whole((count + 8, cells // 2)),
        ]
        + [pl.BlockSpec((size, step), lambda i: (0, i))] * (chunks * parts),
        out_shape=[
            shape((data, cells), jnp.bfloat16),
            shape((data, cells), jnp.bfloat16),
            shape((1, cells), jnp.float32),
            shape((1, data), jnp.float32),
            shape((count + 8, cells // 2), jnp.float32),
        ]
        + [shape((size, data), jnp.float32)] * (chunks * parts),
        scratch_shapes=[
            pltpu.VMEM((count, cells), jnp.float32),
            pltpu.VMEM((count, cells), jnp.float32),
        ],
        compiler_params=pltpu.CompilerParams(vmem_limit_bytes=LIMIT),
        cost_estimate=pl.CostEstimate(
            flops=6 * data * cells * count, bytes_accessed=4 * data * cells, transcendentals=0
        ),
    )(probes, tile, classes, active, coupling)
    blocks = outs[5:]
    return outs[:5], [blocks[i * parts : (i + 1) * parts] for i in range(chunks)]


def turn(high, low):
    def kernel(high, low, high_t, low_t):
        high_t[...] = high[...].T
        low_t[...] = low[...].T

    shape = jax.ShapeDtypeStruct(high.shape[::-1], jnp.bfloat16)
    return call(kernel, [shape, shape], [high, low])


def backward(blocks, high, low):
    def kernel(*refs):
        high, low, own, other = refs[-4:]
        value = jnp.concatenate([ref[...] for ref in refs[:-4]], axis=0)
        back = product(value, high[...], low[...], NN)
        half = own.shape[1]
        own[...] = back[:, :half]
        other[...] = back[:, half:]

    rows = sum(block.shape[0] for block in blocks)
    shape = jax.ShapeDtypeStruct((rows, high.shape[1] // 2), jnp.float32)
    return call(kernel, [shape, shape], [*blocks, high, low], 6 * rows * high.size)


def forward(own, other, mask, high_t, low_t):
    parts = lax.axis_size("cell")

    def kernel(own, other, mask, high_t, low_t, *outs):
        masked = jnp.concatenate([own[...], other[...]], axis=1) * mask[...]
        out = product(masked, high_t[...], low_t[...], NN)
        size = out.shape[0] // parts
        for x, ref in enumerate(outs):
            ref[...] = out[x * size : (x + 1) * size]

    rows = own.shape[0]
    shape = jax.ShapeDtypeStruct((rows // parts, high_t.shape[1]), jnp.float32)
    operands = [own, other, mask, high_t, low_t]
    return call(kernel, [shape] * parts, operands, 6 * rows * high_t.size)


def finish(halves):
    chunks = len(halves)
    parts = lax.axis_size("cell")
    rows, half = halves[0][0].shape
    size = rows // parts

    def kernel(*refs):
        out, turned = refs[-2:]
        side = lax.axis_index("dp") % 2
        here = lax.axis_index("cell")
        own = pl.ds(pl.multiple_of(side * half, half), half)
        other = pl.ds(pl.multiple_of((1 - side) * half, half), half)
        for chunk in range(chunks):
            for x in range(parts):
                start = pl.multiple_of((chunk * parts + (here ^ x)) * size, size)
                block = slice(x * size, (x + 1) * size)
                turned[pl.ds(start, size), own] = refs[2 * chunk][block, :]
                turned[pl.ds(start, size), other] = refs[2 * chunk + 1][block, :]
        out[...] = turned[...].T

    shape = jax.ShapeDtypeStruct((2 * half, chunks * rows), jnp.float32)
    return pl.pallas_call(
        kernel,
        out_shape=shape,
        in_specs=[VMEM] * (2 * chunks),
        out_specs=VMEM,
        scratch_shapes=[pltpu.VMEM(shape.shape[::-1], jnp.float32)],
        compiler_params=pltpu.CompilerParams(vmem_limit_bytes=LIMIT),
    )(*[half for pair in halves for half in pair])


def sum_cells(blocks, weight):
    got = {x: swap(blocks[x], "cell", x) for x in reversed(range(1, len(blocks)))}
    total = blocks[0]
    for x in range(1, len(blocks)):
        total = total + got[x]
    return total * weight


def gather_cells(total):
    parts = lax.axis_size("cell")
    return [total] + [swap(total, "cell", x) for x in range(1, parts)]


def sum_data(own, other):
    total = own + swap(other, "dp", 1)
    stride = 2
    while stride < lax.axis_size("dp"):
        total = total + swap(total, "dp", stride)
        stride *= 2
    return total


def neighbours(message):
    if lax.axis_size("section") == 2:
        got = swap(message, "section", 1)
        return got, got
    return shifted(message, "section", 1), shifted(message, "section", -1)


def local(probes, jacobian, classes, active, coupling):
    probes, tile = probes[0], jacobian[0]
    count, half = probes.shape[1], probes.shape[0] // 2
    parts = lax.axis_size("cell")
    chunks = MAX_CHUNKS
    while chunks > 1 and count % (8 * chunks * parts):
        chunks -= 1
    rows = count // chunks
    sections = lax.axis_size("section")
    section = lax.axis_index("section")

    (high, low, mask, weight, message), blocks = first_forward(
        probes, tile, classes, active, coupling, chunks
    )
    high_t, low_t = turn(high, low)
    mask_own = mask[:, :half]

    below, above = neighbours(message)
    strength = jnp.where(section == 0, 0.0, message[count : count + 1])
    strength_next = jnp.where(section == sections - 1, 0.0, above[count : count + 1])

    def smoothing(masked, below, above):
        return strength * (masked - below) + strength_next * (masked - above)

    def hessian(blocks, smooth):
        back = backward(gather_cells(sum_cells(blocks, weight)), high, low)
        return mask_own * (sum_data(*back) + smooth)

    def part(value, chunk):
        return value[chunk * rows : (chunk + 1) * rows]

    first = []
    for chunk in range(chunks):
        smooth = smoothing(*[part(value, chunk) for value in (message, below, above)])
        own = hessian(blocks[chunk], smooth)
        first.append((own, swap(own, "dp", 1)))
    masked = jnp.concatenate([own for own, _ in first], axis=0) * mask_own
    below, above = neighbours(masked)
    second = []
    for chunk in range(chunks):
        own, other = first[chunk]
        smooth = smoothing(*[part(value, chunk) for value in (masked, below, above)])
        own = hessian(forward(own, other, mask, high_t, low_t), smooth)
        second.append((own, swap(own, "dp", 1)))
    return finish(first)[None], finish(second)[None]


def solution(mesh):
    return jax.shard_map(
        local,
        mesh=mesh,
        in_specs=(
            P("section", "cell", None),
            P("section", "dp", "cell"),
            P("section", "dp"),
            P("section", "cell"),
            P("section", "cell"),
        ),
        out_specs=(P("section", "cell", None), P("section", "cell", None)),
        check_vma=False,
    )
```

```python
import functools

import jax
import jax.numpy as jnp
from jax import lax
from jax.experimental import pallas as pl
from jax.experimental.pallas import tpu as pltpu
from jax.sharding import PartitionSpec as P

MAX_CHUNKS = 2
LIMIT = 16 * 2**20
LARGE = 55 * 2**20
NT = (((1,), (1,)), ((), ()))
NN = (((1,), (0,)), ((), ()))
VMEM = pl.BlockSpec(memory_space=pltpu.VMEM)


def swap(value, axis, stride):
    return lax.ppermute(value, axis, [(i, i ^ stride) for i in range(lax.axis_size(axis))])


def shifted(value, axis, by):
    length = lax.axis_size(axis)
    pairs = [(i, i + by) for i in range(length) if 0 <= i + by < length]
    return lax.ppermute(value, axis, pairs)


def split(value):
    high = value.astype(jnp.bfloat16)
    return high, (value - high.astype(jnp.float32)).astype(jnp.bfloat16)


def product(value, high, low, dims):
    top, rest = split(value)
    rows = value.shape[0]
    dot = functools.partial(
        lax.dot_general, dimension_numbers=dims, preferred_element_type=jnp.float32
    )
    both = dot(jnp.concatenate([top, rest], axis=0), high)
    return both[:rows] + (both[rows:] + dot(top, low))


def call(kernel, shapes, operands, flops=0, scratch=()):
    return pl.pallas_call(
        kernel,
        out_shape=shapes,
        in_specs=[VMEM] * len(operands),
        out_specs=[VMEM] * len(shapes),
        scratch_shapes=scratch,
        compiler_params=pltpu.CompilerParams(vmem_limit_bytes=LIMIT),
        cost_estimate=pl.CostEstimate(
            flops=flops, bytes_accessed=sum(4 * o.size for o in operands), transcendentals=0
        ),
    )(*operands)


def own_first(ref, rows, side, half):
    own = pl.ds(pl.multiple_of(side * half, half), half)
    other = pl.ds(pl.multiple_of((1 - side) * half, half), half)
    return jnp.concatenate([ref[rows, own], ref[rows, other]], axis=1)


def block_order(parts):
    bits = parts.bit_length() - 1
    return [int(format(i, "b").zfill(bits)[::-1], 2) for i in range(parts)]


def first_kernel(chunks, parts, step, *refs):
    probes_hbm, tile_hbm, active_hbm = refs[:3]
    high, low = refs[3:5]
    blocks = refs[5:-5]
    probes, tile, active, turned, arrived = refs[-5:]
    side = lax.axis_index("dp") % 2
    here = lax.axis_index("cell")
    cells, count = probes.shape
    data = tile.shape[0]
    half = cells // 2
    size = count // (chunks * parts)

    pairs = [(active_hbm, active), (probes_hbm, probes)]
    pairs += [
        (tile_hbm.at[pl.ds(at, step)], tile.at[pl.ds(at, step)]) for at in range(0, data, step)
    ]
    copies = [
        pltpu.make_async_copy(source, target, arrived.at[index])
        for index, (source, target) in enumerate(pairs)
    ]
    for copy in copies:
        copy.start()
    copies[0].wait()
    keep = jnp.broadcast_to(active[...].astype(jnp.float32), (8, cells)).T[:, :1]
    copies[1].wait()
    top, rest = split(probes[...] * keep)
    both = jnp.concatenate([top, rest], axis=1)

    left = pl.ds(pl.multiple_of(side * half, half), half)
    right = pl.ds(pl.multiple_of((1 - side) * half, half), half)
    dot = functools.partial(jnp.dot, preferred_element_type=jnp.float32)
    for index, at in enumerate(range(0, data, step)):
        copies[2 + index].wait()
        rows = slice(at, at + step)
        tile_top, tile_rest = split(tile[rows, :])
        for ref, value in ((high, tile_top), (low, tile_rest)):
            ref[rows, left] = value[:, :half]
            ref[rows, right] = value[:, half:]
        out = dot(tile_top, both)
        out = out[:, :count] + (out[:, count:] + dot(tile_rest, top))
        turned[:, rows] = out.T

    for chunk in range(chunks):
        for index, x in enumerate(block_order(parts)):
            start = pl.multiple_of((chunk * parts + (here ^ x)) * size, size)
            block = blocks[2 * chunk + index // (parts // 2)]
            spot = index % (parts // 2) * size
            block[spot : spot + size, :] = turned[pl.ds(start, size), :]


def first_forward(probes, tile, active, chunks):
    parts = lax.axis_size("cell")
    cells, count = probes.shape
    data = tile.shape[0]
    step = 256 if data % 256 == 0 else data
    operands = [probes, tile, active]
    shapes = [pltpu.VMEM((data, cells), jnp.bfloat16)] * 2
    shapes += [jax.ShapeDtypeStruct((count // (2 * chunks), data), jnp.float32)] * (2 * chunks)
    outs = pl.pallas_call(
        functools.partial(first_kernel, chunks, parts, step),
        in_specs=[pl.BlockSpec(memory_space=pltpu.HBM)] * len(operands),
        out_specs=[VMEM] * len(shapes),
        out_shape=shapes,
        scratch_shapes=[pltpu.VMEM(o.shape, o.dtype) for o in operands]
        + [pltpu.VMEM((count, data), jnp.float32), pltpu.SemaphoreType.DMA((data // step + 2,))],
        compiler_params=pltpu.CompilerParams(vmem_limit_bytes=LARGE),
        cost_estimate=pl.CostEstimate(
            flops=6 * data * cells * count, bytes_accessed=4 * data * cells, transcendentals=0
        ),
    )(*operands)
    return outs[:2], [outs[2 + 2 * i : 4 + 2 * i] for i in range(chunks)]


def prepare(probes, classes, active, coupling, chunks):
    parts = lax.axis_size("cell")
    cells, count = probes.shape
    half = cells // 2
    size = count // (chunks * parts)
    every = slice(None)

    def kernel(probes, classes, active, coupling, *refs):
        mask, weight, message, turned = refs
        side = lax.axis_index("dp") % 2
        here = lax.axis_index("cell")
        keep = own_first(active, every, side, half).astype(jnp.float32)
        mask[...] = keep
        turned[...] = probes[...].T
        own = pl.ds(pl.multiple_of(side * half, half), half)
        for chunk in range(chunks):
            for index, x in enumerate(block_order(parts)):
                spot = (chunk * parts + index) * size
                start = pl.multiple_of((chunk * parts + (here ^ x)) * size, size)
                message[spot : spot + size, :] = turned[pl.ds(start, size), own] * keep[:, :half]
        message[count:, :] = jnp.broadcast_to(coupling[:, own], (8, half))
        labels = classes[...]
        weight[...] = jnp.where(
            labels == 0, 1.0, jnp.where(labels == 1, 0.5, jnp.where(labels == 2, 0.25, 0.125))
        ).astype(jnp.float32)

    shapes = [
        jax.ShapeDtypeStruct((1, cells), jnp.float32),
        jax.ShapeDtypeStruct(classes.shape, jnp.float32),
        jax.ShapeDtypeStruct((count + 8, half), jnp.float32),
    ]
    operands = [probes, classes, active, coupling]
    scratch = [pltpu.VMEM((count, cells), jnp.float32)]
    return call(kernel, shapes, operands, scratch=scratch)


def turn(high, low):
    def kernel(high, low, high_t, low_t):
        high_t[...] = high[...].T
        low_t[...] = low[...].T

    shape = jax.ShapeDtypeStruct(high.shape[::-1], jnp.bfloat16)
    return call(kernel, [shape, shape], [high, low])


def backward(blocks, high, low):
    def kernel(*refs):
        high, low, own, other = refs[-4:]
        value = jnp.concatenate([ref[...] for ref in refs[:-4]], axis=0)
        back = product(value, high[...], low[...], NN)
        half = own.shape[1]
        own[...] = back[:, :half]
        other[...] = back[:, half:]

    rows = sum(block.shape[0] for block in blocks)
    shape = jax.ShapeDtypeStruct((rows, high.shape[1] // 2), jnp.float32)
    return call(kernel, [shape, shape], [*blocks, high, low], 6 * rows * high.size)


def forward(own, other, mask, high_t, low_t):
    def kernel(own, other, mask, high_t, low_t, keep, send):
        masked = jnp.concatenate([own[...], other[...]], axis=1) * mask[...]
        out = product(masked, high_t[...], low_t[...], NN)
        size = out.shape[0] // 2
        keep[...] = out[:size]
        send[...] = out[size:]

    rows = own.shape[0]
    shape = jax.ShapeDtypeStruct((rows // 2, high_t.shape[1]), jnp.float32)
    operands = [own, other, mask, high_t, low_t]
    return call(kernel, [shape, shape], operands, 6 * rows * high_t.size)


def finish(halves):
    chunks = len(halves) // 2
    parts = lax.axis_size("cell")
    rows, half = halves[0].shape
    size = rows // parts

    def kernel(*refs):
        out, turned = refs[-2:]
        side = lax.axis_index("dp") % 2
        here = lax.axis_index("cell")
        own = pl.ds(pl.multiple_of(side * half, half), half)
        other = pl.ds(pl.multiple_of((1 - side) * half, half), half)
        for chunk in range(chunks):
            for index, x in enumerate(block_order(parts)):
                start = pl.multiple_of((chunk * parts + (here ^ x)) * size, size)
                block = slice(index * size, (index + 1) * size)
                turned[pl.ds(start, size), own] = refs[2 * chunk][block, :]
                turned[pl.ds(start, size), other] = refs[2 * chunk + 1][block, :]
        out[...] = turned[...].T

    shape = jax.ShapeDtypeStruct((2 * half, chunks * rows), jnp.float32)
    return pl.pallas_call(
        kernel,
        out_shape=shape,
        in_specs=[VMEM] * (2 * chunks),
        out_specs=VMEM,
        scratch_shapes=[pltpu.VMEM(shape.shape[::-1], jnp.float32)],
        compiler_params=pltpu.CompilerParams(vmem_limit_bytes=LIMIT),
    )(*halves)


def sum_cells(keep, send, shared):
    parts = lax.axis_size("cell")
    value = yield (lambda a, b: a + b), keep, swap(send, "cell", 1)
    half = value.shape[0] // 2
    stride = 2
    while stride < parts // 2:
        value = value[:half] + swap(value[half:], "cell", stride)
        half //= 2
        stride *= 2
    other = swap(jnp.concatenate([value[half:], value[:half]], axis=0), "cell", stride)
    value = yield (lambda a, b: (a + b) * shared["weight"]), value, other
    while stride > 2:
        stride //= 2
        value = jnp.concatenate([value, swap(value, "cell", stride)], axis=0)
    return value, swap(value, "cell", 1)


def sum_data(own, other):
    total = yield (lambda a, b: a + b), own, swap(other, "dp", 1)
    stride = 2
    while stride < lax.axis_size("dp") // 2:
        total = total + swap(total, "dp", stride)
        stride *= 2
    return total, swap(total, "dp", stride)


def in_turn(chains):
    results = [None] * len(chains)
    answers = [None] * len(chains)
    token = None
    waiting = list(range(len(chains)))
    while waiting:
        for index in list(waiting):
            try:
                step = chains[index].send(answers[index])
            except StopIteration as stop:
                results[index] = stop.value
                waiting.remove(index)
                continue
            if step is None:
                answers[index] = None
                continue
            function, *values = step
            if token is not None:
                *values, _ = lax.optimization_barrier((*values, token))
            answers[index] = function(*values)
            token = jax.tree.leaves(answers[index])[0]
    return results


def neighbours(message):
    if lax.axis_size("section") == 2:
        got = swap(message, "section", 1)
        return got, got
    return shifted(message, "section", 1), shifted(message, "section", -1)


def local(probes, jacobian, classes, active, coupling):
    probes, tile = probes[0], jacobian[0]
    count, half = probes.shape[1], probes.shape[0] // 2
    parts = lax.axis_size("cell")
    chunks = MAX_CHUNKS
    while chunks > 1 and count % (8 * chunks * parts):
        chunks -= 1
    rows = count // chunks
    sections = lax.axis_size("section")
    section = lax.axis_index("section")

    (high, low), blocks = first_forward(probes, tile, active, chunks)
    shared = {}

    def ready(*operands):
        mask, weight, message = prepare(*operands, chunks)
        below, above = neighbours(message)
        strength = jnp.where(section == 0, 0.0, message[count : count + 1])
        strength_next = jnp.where(section == sections - 1, 0.0, above[count : count + 1])
        shared.update(mask=mask, mask_own=mask[:, :half], weight=weight)
        shared.update(first=(message, below, above), strength=(strength, strength_next))
        return mask

    def turned(high, low):
        shared["turned"] = turn(high, low)
        return shared["turned"]

    def part(value, chunk):
        return value[chunk * rows : (chunk + 1) * rows]

    def smoothing(here, under, over):
        strength, strength_next = shared["strength"]
        return strength * (here - under) + strength_next * (here - over)

    def hessian(keep, send, smooth):
        sent = yield from sum_cells(keep, send, shared)
        own, other = yield (lambda *values: backward(values, high, low)), *sent
        total, other = yield from sum_data(own, other)
        own = yield (lambda a, b: shared["mask_own"] * (a + b + smooth())), total, other
        return own, swap(own, "dp", 1)

    def chain(chunk):
        def smooth_first():
            return smoothing(*[part(value, chunk) for value in shared["first"]])

        image = yield from hessian(*blocks[chunk], smooth_first)
        shared[chunk] = image

        def smooth_second():
            if "masked" not in shared:
                masked = jnp.concatenate([shared[i][0] for i in range(chunks)], axis=0)
                masked = masked * shared["mask_own"]
                shared["masked"] = (masked, *neighbours(masked))
            return smoothing(*[part(value, chunk) for value in shared["masked"]])

        sent = yield (lambda a, b: forward(a, b, shared["mask"], *shared["turned"])), *image
        return (yield from hessian(*sent, smooth_second))

    def aside():
        yield ready, probes, classes, active, coupling
        yield None
        yield None
        yield None
        yield turned, high, low
        yield None
        halves = [value for chunk in range(chunks) for value in shared[chunk]]
        return (yield (lambda *values: finish(values)), *halves)

    start, first, *rest = in_turn([chain(0), aside()] + [chain(chunk) for chunk in range(1, chunks)])
    second = finish([half for halves in (start, *rest) for half in halves])
    return first[None], second[None]


def solution(mesh):
    return jax.shard_map(
        local,
        mesh=mesh,
        in_specs=(
            P("section", "cell", None),
            P("section", "dp", "cell"),
            P("section", "dp"),
            P("section", "cell"),
            P("section", "cell"),
        ),
        out_specs=(P("section", "cell", None), P("section", "cell", None)),
        check_vma=False,
    )
```

```python
import functools

import jax
import jax.numpy as jnp
from jax import lax
from jax.experimental import pallas as pl
from jax.experimental.pallas import tpu as pltpu
from jax.sharding import PartitionSpec as P

MAX_CHUNKS = 2
LIMIT = 16 * 2**20
LARGE = 16 * 2**20
NT = (((1,), (1,)), ((), ()))
NN = (((1,), (0,)), ((), ()))
VMEM = pl.BlockSpec(memory_space=pltpu.VMEM)


def swap(value, axis, stride):
    return lax.ppermute(value, axis, [(i, i ^ stride) for i in range(lax.axis_size(axis))])


def shifted(value, axis, by):
    length = lax.axis_size(axis)
    pairs = [(i, i + by) for i in range(length) if 0 <= i + by < length]
    return lax.ppermute(value, axis, pairs)


def class_weight(labels):
    return jnp.where(
        labels == 0, 1.0, jnp.where(labels == 1, 0.5, jnp.where(labels == 2, 0.25, 0.125))
    ).astype(jnp.float32)


def split(value):
    high = value.astype(jnp.bfloat16)
    return high, (value - high.astype(jnp.float32)).astype(jnp.bfloat16)


def product(value, high, low, dims):
    top, rest = split(value)
    rows = value.shape[0]
    dot = functools.partial(
        lax.dot_general, dimension_numbers=dims, preferred_element_type=jnp.float32
    )
    both = dot(jnp.concatenate([top, rest], axis=0), high)
    return both[:rows] + (both[rows:] + dot(top, low))


def call(kernel, shapes, operands, flops=0, scratch=()):
    return pl.pallas_call(
        kernel,
        out_shape=shapes,
        in_specs=[VMEM] * len(operands),
        out_specs=[VMEM] * len(shapes),
        scratch_shapes=scratch,
        compiler_params=pltpu.CompilerParams(vmem_limit_bytes=LIMIT),
        cost_estimate=pl.CostEstimate(
            flops=flops, bytes_accessed=sum(4 * o.size for o in operands), transcendentals=0
        ),
    )(*operands)


def sides(first, second):
    left = lax.axis_index("dp") % 2 == 0
    return jnp.where(left, first, second), jnp.where(left, second, first)


def block_order(parts):
    bits = parts.bit_length() - 1
    return [int(format(i, "b").zfill(bits)[::-1], 2) for i in range(parts)]


def column(active):
    cells = active.shape[1]
    return jnp.broadcast_to(active[...].astype(jnp.float32), (8, cells)).T[:, :1]


def place(turned, parts, keep, send):
    here = lax.axis_index("cell")
    size = turned.shape[0] // parts
    for index, x in enumerate(block_order(parts)):
        start = pl.multiple_of((here ^ x) * size, size)
        block = send if index // (parts // 2) else keep
        spot = index % (parts // 2) * size
        block[spot : spot + size, :] = turned[pl.ds(start, size), :]


def rows_product(high, low, both):
    count = both.shape[1] // 2
    dot = functools.partial(jnp.dot, preferred_element_type=jnp.float32)
    out = dot(high, both)
    return out[:, :count] + (out[:, count:] + dot(low, both[:, :count]))


def column(active):
    cells = active.shape[1]
    return jnp.broadcast_to(active[...].astype(jnp.float32), (8, cells)).T[:, :1]


def rows_product(high, low, both):
    count = both.shape[1] // 2
    dot = functools.partial(jnp.dot, preferred_element_type=jnp.float32)
    out = dot(high, both)
    return out[:, :count] + (out[:, count:] + dot(low, both[:, :count]))


def first_forward(probes, tile, active, coupling, chunks):
    parts = lax.axis_size("cell")
    cells, count = probes.shape
    data = tile.shape[0]
    half = cells // 2
    rows = count // chunks
    size = rows // parts
    step = 512 if data % 512 == 0 else data

    def kernel(probes_hbm, tile_hbm, active_hbm, coupling_hbm, high, low, message, factors, *refs):
        blocks, (probes, tile, active, coupling, turned, masked, arrived) = refs[:-7], refs[-7:]
        pairs = [(active_hbm, active), (probes_hbm, probes)]
        pairs += [
            (tile_hbm.at[pl.ds(at, step)], tile.at[pl.ds(at, step)]) for at in range(0, data, step)
        ]
        pairs += [(coupling_hbm, coupling)]
        copies = [
            pltpu.make_async_copy(source, target, arrived.at[index])
            for index, (source, target) in enumerate(pairs)
        ]
        for copy in copies:
            copy.start()
        copies[0].wait()
        mask = column(active)
        copies[1].wait()
        values = probes[...] * mask
        both = jnp.concatenate(split(values), axis=1)
        masked[...] = values.T
        for index, at in enumerate(range(0, data, step)):
            copies[2 + index].wait()
            block = slice(at, at + step)
            top, rest = split(tile[block, :])
            high[block, :] = top
            low[block, :] = rest
            turned[:, block] = rows_product(top, rest, both).T
        copies[-1].wait()
        here = lax.axis_index("cell")
        own = pl.ds(pl.multiple_of(lax.axis_index("dp") % 2 * half, half), half)
        for chunk in range(chunks):
            for index, x in enumerate(block_order(parts)):
                start = pl.multiple_of((chunk * parts + (here ^ x)) * size, size)
                block = blocks[2 * chunk + index // (parts // 2)]
                spot = index % (parts // 2) * size
                block[spot : spot + size, :] = turned[pl.ds(start, size), :]
                spot = (chunk * parts + index) * size
                message[spot : spot + size, :] = masked[pl.ds(start, size), own]
        message[count:, :] = jnp.broadcast_to(coupling[:, own], (8, half))
        section = lax.axis_index("section")
        last = lax.axis_size("section") - 1
        keep = active[:, own].astype(jnp.float32)
        zero = jnp.zeros_like(keep)
        factors[0:1, :] = keep
        factors[1:2, :] = jnp.where(section == 0, zero, coupling[:, own])
        factors[2:3, :] = jnp.where(section == last, zero, zero + 1.0)

    operands = [pltpu.with_memory_space_constraint(o, pltpu.HBM) for o in (probes, tile, active, coupling)]
    shapes = [pltpu.VMEM((data, cells), jnp.bfloat16)] * 2
    shapes += [jax.ShapeDtypeStruct((count + 8, half), jnp.float32)]
    shapes += [jax.ShapeDtypeStruct((8, half), jnp.float32)]
    shapes += [jax.ShapeDtypeStruct((rows // 2, data), jnp.float32)] * (2 * chunks)
    outs = pl.pallas_call(
        kernel,
        in_specs=[pl.BlockSpec(memory_space=pltpu.HBM)] * len(operands),
        out_specs=[VMEM] * len(shapes),
        out_shape=shapes,
        scratch_shapes=[pltpu.VMEM(o.shape, o.dtype) for o in operands]
        + [
            pltpu.VMEM((count, data), jnp.float32),
            pltpu.VMEM((count, cells), jnp.float32),
            pltpu.SemaphoreType.DMA((data // step + 3,)),
        ],
        compiler_params=pltpu.CompilerParams(vmem_limit_bytes=LARGE),
        cost_estimate=pl.CostEstimate(
            flops=6 * data * cells * count, bytes_accessed=4 * data * cells, transcendentals=0
        ),
    )(*operands)
    return outs[:4], [outs[4 + 2 * i : 6 + 2 * i] for i in range(chunks)]


def turn(high, low):
    def kernel(high, low, high_t, low_t):
        high_t[...] = high[...].T
        low_t[...] = low[...].T

    shape = jax.ShapeDtypeStruct(high.shape[::-1], jnp.bfloat16)
    return call(kernel, [shape, shape], [high, low])


def backward(blocks, high, low):
    def kernel(*refs):
        high, low, own, other = refs[-4:]
        value = jnp.concatenate([ref[...] for ref in refs[:-4]], axis=0)
        back = product(value, high[...], low[...], NN)
        half = own.shape[1]
        own[...], other[...] = sides(back[:, :half], back[:, half:])

    rows = sum(block.shape[0] for block in blocks)
    shape = jax.ShapeDtypeStruct((rows, high.shape[1] // 2), jnp.float32)
    return call(kernel, [shape, shape], [*blocks, high, low], 6 * rows * high.size)


def forward(own, other, mask, high_t, low_t):
    def kernel(own, other, mask, high_t, low_t, keep, send):
        masked = jnp.concatenate(sides(own[...], other[...]), axis=1) * mask[...]
        out = product(masked, high_t[...], low_t[...], NN)
        size = out.shape[0] // 2
        keep[...] = out[:size]
        send[...] = out[size:]

    rows = own.shape[0]
    shape = jax.ShapeDtypeStruct((rows // 2, high_t.shape[1]), jnp.float32)
    operands = [own, other, mask, high_t, low_t]
    return call(kernel, [shape, shape], operands, 6 * rows * high_t.size)


def finish(halves):
    chunks = len(halves) // 2
    parts = lax.axis_size("cell")
    rows, half = halves[0].shape
    size = rows // parts

    def kernel(*refs):
        out, turned = refs[-2:]
        side = lax.axis_index("dp") % 2
        here = lax.axis_index("cell")
        own = pl.ds(pl.multiple_of(side * half, half), half)
        other = pl.ds(pl.multiple_of((1 - side) * half, half), half)
        for chunk in range(chunks):
            for index, x in enumerate(block_order(parts)):
                start = pl.multiple_of((chunk * parts + (here ^ x)) * size, size)
                block = slice(index * size, (index + 1) * size)
                turned[pl.ds(start, size), own] = refs[2 * chunk][block, :]
                turned[pl.ds(start, size), other] = refs[2 * chunk + 1][block, :]
        out[...] = turned[...].T

    shape = jax.ShapeDtypeStruct((2 * half, chunks * rows), jnp.float32)
    return pl.pallas_call(
        kernel,
        out_shape=shape,
        in_specs=[VMEM] * (2 * chunks),
        out_specs=VMEM,
        scratch_shapes=[pltpu.VMEM(shape.shape[::-1], jnp.float32)],
        compiler_params=pltpu.CompilerParams(vmem_limit_bytes=LIMIT),
    )(*halves)


def sum_cells(keep, send, shared):
    parts = lax.axis_size("cell")
    value = yield (lambda a, b: a + b), keep, swap(send, "cell", 1)
    half = value.shape[0] // 2
    stride = 2
    while stride < parts // 2:
        value = value[:half] + swap(value[half:], "cell", stride)
        half //= 2
        stride *= 2
    other = swap(jnp.concatenate([value[half:], value[:half]], axis=0), "cell", stride)
    value = yield (lambda a, b: (a + b) * shared["weight"]), value, other
    while stride > 2:
        stride //= 2
        value = jnp.concatenate([value, swap(value, "cell", stride)], axis=0)
    return value, swap(value, "cell", 1)


def sum_data(own, other):
    total = yield (lambda a, b: a + b), own, swap(other, "dp", 1)
    stride = 2
    while stride < lax.axis_size("dp") // 2:
        total = total + swap(total, "dp", stride)
        stride *= 2
    return total, swap(total, "dp", stride)


def in_turn(chains, rounds):
    results = [None] * len(chains)
    answers = [None] * len(chains)
    token = None
    waiting = list(range(len(chains)))
    while waiting:
        steps = rounds[0]
        rounds = rounds[1:] + rounds[:1]
        for index, (chain, single) in enumerate(chains):
            for _ in range(1 if single else steps):
                if index not in waiting:
                    break
                try:
                    step = chain.send(answers[index])
                except StopIteration as stop:
                    results[index] = stop.value
                    waiting.remove(index)
                    break
                answers[index] = None
                if step is None:
                    continue
                function, *values = step
                if token is not None:
                    *values, _ = lax.optimization_barrier((*values, token))
                answers[index] = function(*values)
                token = jax.tree.leaves(answers[index])[0]
    return results


def neighbours(message):
    if lax.axis_size("section") == 2:
        got = swap(message, "section", 1)
        return got, got
    return shifted(message, "section", 1), shifted(message, "section", -1)


def local(probes, jacobian, classes, active, coupling):
    probes, tile = probes[0], jacobian[0]
    count, half = probes.shape[1], probes.shape[0] // 2
    parts = lax.axis_size("cell")
    chunks = MAX_CHUNKS
    while chunks > 1 and count % (8 * chunks * parts):
        chunks -= 1
    rows = count // chunks

    (high, low, message, factors), blocks = first_forward(probes, tile, active, coupling, chunks)
    shared = {"mask": active.astype(jnp.float32), "mask_own": factors[:1]}
    shared["weight"] = class_weight(classes)

    def ready(message):
        below, above = neighbours(message)
        shared.update(first=(message, below, above))
        shared.update(strength=(factors[1:2], factors[2:3] * above[count : count + 1]))
        return message

    def turned(high, low):
        shared["turned"] = turn(high, low)
        return shared["turned"]

    def part(value, chunk):
        return value[chunk * rows : (chunk + 1) * rows]

    def smoothing(here, under, over):
        strength, strength_next = shared["strength"]
        return strength * (here - under) + strength_next * (here - over)

    def hessian(keep, send, smooth):
        sent = yield from sum_cells(keep, send, shared)
        own, other = yield (lambda *values: backward(values, high, low)), *sent
        total, other = yield from sum_data(own, other)
        own = yield (lambda a, b: shared["mask_own"] * (a + b + smooth())), total, other
        return own, swap(own, "dp", 1)

    def second_message(*halves):
        masked = jnp.concatenate(halves, axis=0) * shared["mask_own"]
        shared["second"] = (masked, *neighbours(masked))
        return masked

    def chain(chunk):
        def smooth_first():
            return smoothing(*[part(value, chunk) for value in shared["first"]])

        image = yield from hessian(*blocks[chunk], smooth_first)
        shared[chunk] = image

        def smooth_second():
            return smoothing(*[part(value, chunk) for value in shared["second"]])

        sent = yield (lambda a, b: forward(a, b, shared["mask"], *shared["turned"])), *image
        return (yield from hessian(*sent, smooth_second))

    def between():
        yield None
        yield None
        yield None
        yield None
        yield None
        halves = [value for chunk in range(chunks) for value in shared[chunk]]
        return (yield (lambda *values: finish(values)), *halves)

    def after():
        yield ready, message
        yield None
        yield turned, high, low
        yield None
        yield None
        yield second_message, *[shared[chunk][0] for chunk in range(chunks)]

    chains = [(chain(chunk), False) for chunk in range(chunks)]
    chains[1:1] = [(between(), True)]
    halves, first, *rest = in_turn(chains + [(after(), True)], (1, 1, 2, 1, 1))
    for more in rest[:-1]:
        halves = halves + more
    return first[None], finish(halves)[None]


def solution(mesh):
    return jax.shard_map(
        local,
        mesh=mesh,
        in_specs=(
            P("section", "cell", None),
            P("section", "dp", "cell"),
            P("section", "dp"),
            P("section", "cell"),
            P("section", "cell"),
        ),
        out_specs=(P("section", "cell", None), P("section", "cell", None)),
        check_vma=False,
    )
```

```python
import functools

import jax
import jax.numpy as jnp
from jax import lax
from jax.experimental import pallas as pl
from jax.experimental.pallas import tpu as pltpu
from jax.sharding import PartitionSpec as P

MAX_CHUNKS = 2
LIMIT = 16 * 2**20
LARGE = 16 * 2**20
NT = (((1,), (1,)), ((), ()))
NN = (((1,), (0,)), ((), ()))
VMEM = pl.BlockSpec(memory_space=pltpu.VMEM)


def swap(value, axis, stride):
    return lax.ppermute(value, axis, [(i, i ^ stride) for i in range(lax.axis_size(axis))])


def shifted(value, axis, by):
    length = lax.axis_size(axis)
    pairs = [(i, i + by) for i in range(length) if 0 <= i + by < length]
    return lax.ppermute(value, axis, pairs)


def class_weight(labels):
    return jnp.where(
        labels == 0, 1.0, jnp.where(labels == 1, 0.5, jnp.where(labels == 2, 0.25, 0.125))
    ).astype(jnp.float32)


def split(value):
    high = value.astype(jnp.bfloat16)
    return high, (value - high.astype(jnp.float32)).astype(jnp.bfloat16)


def product(value, high, low, dims):
    top, rest = split(value)
    rows = value.shape[0]
    dot = functools.partial(
        lax.dot_general, dimension_numbers=dims, preferred_element_type=jnp.float32
    )
    both = dot(jnp.concatenate([top, rest], axis=0), high)
    return both[:rows] + (both[rows:] + dot(top, low))


def call(kernel, shapes, operands, flops=0, scratch=()):
    return pl.pallas_call(
        kernel,
        out_shape=shapes,
        in_specs=[VMEM] * len(operands),
        out_specs=[VMEM] * len(shapes),
        scratch_shapes=scratch,
        compiler_params=pltpu.CompilerParams(vmem_limit_bytes=LIMIT),
        cost_estimate=pl.CostEstimate(
            flops=flops, bytes_accessed=sum(4 * o.size for o in operands), transcendentals=0
        ),
    )(*operands)


def sides(first, second):
    left = lax.axis_index("dp") % 2 == 0
    return jnp.where(left, first, second), jnp.where(left, second, first)


def block_order(parts):
    bits = parts.bit_length() - 1
    return [int(format(i, "b").zfill(bits)[::-1], 2) for i in range(parts)]


def column(active):
    cells = active.shape[1]
    return jnp.broadcast_to(active[...].astype(jnp.float32), (8, cells)).T[:, :1]


def place(turned, parts, keep, send):
    here = lax.axis_index("cell")
    size = turned.shape[0] // parts
    for index, x in enumerate(block_order(parts)):
        start = pl.multiple_of((here ^ x) * size, size)
        block = send if index // (parts // 2) else keep
        spot = index % (parts // 2) * size
        block[spot : spot + size, :] = turned[pl.ds(start, size), :]


def rows_product(high, low, both):
    count = both.shape[1] // 2
    dot = functools.partial(jnp.dot, preferred_element_type=jnp.float32)
    out = dot(high, both)
    return out[:, :count] + (out[:, count:] + dot(low, both[:, :count]))


def column(active):
    cells = active.shape[1]
    return jnp.broadcast_to(active[...].astype(jnp.float32), (8, cells)).T[:, :1]


def rows_product(high, low, both):
    count = both.shape[1] // 2
    dot = functools.partial(jnp.dot, preferred_element_type=jnp.float32)
    out = dot(high, both)
    return out[:, :count] + (out[:, count:] + dot(low, both[:, :count]))


def first_forward(probes, tile, active, coupling, chunks):
    parts = lax.axis_size("cell")
    cells, count = probes.shape
    data = tile.shape[0]
    half = cells // 2
    rows = count // chunks
    size = rows // parts
    step = 512 if data % 512 == 0 else data

    def kernel(probes_hbm, tile_hbm, active_hbm, coupling_hbm, high, low, message, factors, *refs):
        blocks, (probes, tile, active, coupling, turned, masked, arrived) = refs[:-7], refs[-7:]
        pairs = [(active_hbm, active), (probes_hbm, probes)]
        pairs += [
            (tile_hbm.at[pl.ds(at, step)], tile.at[pl.ds(at, step)]) for at in range(0, data, step)
        ]
        pairs += [(coupling_hbm, coupling)]
        copies = [
            pltpu.make_async_copy(source, target, arrived.at[index])
            for index, (source, target) in enumerate(pairs)
        ]
        for copy in copies:
            copy.start()
        copies[0].wait()
        mask = column(active)
        copies[1].wait()
        values = probes[...] * mask
        both = jnp.concatenate(split(values), axis=1)
        masked[...] = values.T
        for index, at in enumerate(range(0, data, step)):
            copies[2 + index].wait()
            block = slice(at, at + step)
            top, rest = split(tile[block, :])
            high[block, :] = top
            low[block, :] = rest
            turned[:, block] = rows_product(top, rest, both).T
        copies[-1].wait()
        here = lax.axis_index("cell")
        own = pl.ds(pl.multiple_of(lax.axis_index("dp") % 2 * half, half), half)
        for chunk in range(chunks):
            for index, x in enumerate(block_order(parts)):
                start = pl.multiple_of((chunk * parts + (here ^ x)) * size, size)
                block = blocks[2 * chunk + index // (parts // 2)]
                spot = index % (parts // 2) * size
                block[spot : spot + size, :] = turned[pl.ds(start, size), :]
                spot = (chunk * parts + index) * size
                message[spot : spot + size, :] = masked[pl.ds(start, size), own]
        message[count:, :] = jnp.broadcast_to(coupling[:, own], (8, half))
        section = lax.axis_index("section")
        last = lax.axis_size("section") - 1
        keep = active[:, own].astype(jnp.float32)
        zero = jnp.zeros_like(keep)
        factors[0:1, :] = keep
        factors[1:2, :] = jnp.where(section == 0, zero, coupling[:, own])
        factors[2:3, :] = jnp.where(section == last, zero, zero + 1.0)

    operands = [pltpu.with_memory_space_constraint(o, pltpu.HBM) for o in (probes, tile, active, coupling)]
    shapes = [pltpu.VMEM((data, cells), jnp.bfloat16)] * 2
    shapes += [jax.ShapeDtypeStruct((count + 8, half), jnp.float32)]
    shapes += [jax.ShapeDtypeStruct((8, half), jnp.float32)]
    shapes += [jax.ShapeDtypeStruct((rows // 2, data), jnp.float32)] * (2 * chunks)
    outs = pl.pallas_call(
        kernel,
        in_specs=[pl.BlockSpec(memory_space=pltpu.HBM)] * len(operands),
        out_specs=[VMEM] * len(shapes),
        out_shape=shapes,
        scratch_shapes=[pltpu.VMEM(o.shape, o.dtype) for o in operands]
        + [
            pltpu.VMEM((count, data), jnp.float32),
            pltpu.VMEM((count, cells), jnp.float32),
            pltpu.SemaphoreType.DMA((data // step + 3,)),
        ],
        compiler_params=pltpu.CompilerParams(vmem_limit_bytes=LARGE),
        cost_estimate=pl.CostEstimate(
            flops=6 * data * cells * count, bytes_accessed=4 * data * cells, transcendentals=0
        ),
    )(*operands)
    return outs[:4], [outs[4 + 2 * i : 6 + 2 * i] for i in range(chunks)]


def turn(high, low):
    def kernel(high, low, high_t, low_t):
        high_t[...] = high[...].T
        low_t[...] = low[...].T

    shape = jax.ShapeDtypeStruct(high.shape[::-1], jnp.bfloat16)
    return call(kernel, [shape, shape], [high, low])


def backward(blocks, high, low):
    def kernel(*refs):
        high, low, own, other = refs[-4:]
        value = jnp.concatenate([ref[...] for ref in refs[:-4]], axis=0)
        back = product(value, high[...], low[...], NN)
        half = own.shape[1]
        own[...], other[...] = sides(back[:, :half], back[:, half:])

    rows = sum(block.shape[0] for block in blocks)
    shape = jax.ShapeDtypeStruct((rows, high.shape[1] // 2), jnp.float32)
    return call(kernel, [shape, shape], [*blocks, high, low], 6 * rows * high.size)


def half_of(ref, mine, axis):
    half = ref.shape[axis] // 2
    side = lax.axis_index("dp") % 2
    side = side if mine else 1 - side
    spot = pl.ds(pl.multiple_of(side * half, half), half)
    return ref[:, spot] if axis else ref[spot, :]


def forward_own(own, mask, high_t, low_t):
    def kernel(own, mask, high_t, low_t, out):
        masked = own[...] * half_of(mask, True, 1)
        out[...] = product(masked, half_of(high_t, True, 0), half_of(low_t, True, 0), NN)

    shape = jax.ShapeDtypeStruct((own.shape[0], high_t.shape[1]), jnp.float32)
    return call(kernel, [shape], [own, mask, high_t, low_t], 3 * own.shape[0] * high_t.size)[0]


def forward(partial, other, mask, high_t, low_t):
    def kernel(partial, other, mask, high_t, low_t, keep, send):
        masked = other[...] * half_of(mask, False, 1)
        out = product(masked, half_of(high_t, False, 0), half_of(low_t, False, 0), NN)
        out = partial[...] + out
        size = out.shape[0] // 2
        keep[...] = out[:size]
        send[...] = out[size:]

    rows = other.shape[0]
    shape = jax.ShapeDtypeStruct((rows // 2, high_t.shape[1]), jnp.float32)
    operands = [partial, other, mask, high_t, low_t]
    return call(kernel, [shape, shape], operands, 3 * rows * high_t.size)


def finish(halves):
    chunks = len(halves) // 2
    parts = lax.axis_size("cell")
    rows, half = halves[0].shape
    size = rows // parts

    def kernel(*refs):
        out, turned = refs[-2:]
        side = lax.axis_index("dp") % 2
        here = lax.axis_index("cell")
        own = pl.ds(pl.multiple_of(side * half, half), half)
        other = pl.ds(pl.multiple_of((1 - side) * half, half), half)
        for chunk in range(chunks):
            for index, x in enumerate(block_order(parts)):
                start = pl.multiple_of((chunk * parts + (here ^ x)) * size, size)
                block = slice(index * size, (index + 1) * size)
                turned[pl.ds(start, size), own] = refs[2 * chunk][block, :]
                turned[pl.ds(start, size), other] = refs[2 * chunk + 1][block, :]
        out[...] = turned[...].T

    shape = jax.ShapeDtypeStruct((2 * half, chunks * rows), jnp.float32)
    return pl.pallas_call(
        kernel,
        out_shape=shape,
        in_specs=[VMEM] * (2 * chunks),
        out_specs=VMEM,
        scratch_shapes=[pltpu.VMEM(shape.shape[::-1], jnp.float32)],
        compiler_params=pltpu.CompilerParams(vmem_limit_bytes=LIMIT),
    )(*halves)


def sum_cells(keep, send, shared):
    parts = lax.axis_size("cell")
    value = yield (lambda a, b: a + b), keep, swap(send, "cell", 1)
    half = value.shape[0] // 2
    stride = 2
    while stride < parts // 2:
        value = value[:half] + swap(value[half:], "cell", stride)
        half //= 2
        stride *= 2
    other = swap(jnp.concatenate([value[half:], value[:half]], axis=0), "cell", stride)
    value = yield (lambda a, b: (a + b) * shared["weight"]), value, other
    while stride > 2:
        stride //= 2
        value = jnp.concatenate([value, swap(value, "cell", stride)], axis=0)
    return value, swap(value, "cell", 1)


def sum_data(own, other):
    total = yield (lambda a, b: a + b), own, swap(other, "dp", 1)
    stride = 2
    while stride < lax.axis_size("dp") // 2:
        total = total + swap(total, "dp", stride)
        stride *= 2
    return total, swap(total, "dp", stride)


def in_turn(chains, rounds):
    results = [None] * len(chains)
    answers = [None] * len(chains)
    token = None
    waiting = list(range(len(chains)))
    while waiting:
        steps = rounds[0]
        rounds = rounds[1:] + rounds[:1]
        for index, (chain, single) in enumerate(chains):
            for _ in range(1 if single else steps):
                if index not in waiting:
                    break
                try:
                    step = chain.send(answers[index])
                except StopIteration as stop:
                    results[index] = stop.value
                    waiting.remove(index)
                    break
                answers[index] = None
                if step is None:
                    continue
                function, *values = step
                if token is not None:
                    *values, _ = lax.optimization_barrier((*values, token))
                answers[index] = function(*values)
                token = jax.tree.leaves(answers[index])[0]
    return results


def neighbours(message):
    if lax.axis_size("section") == 2:
        got = swap(message, "section", 1)
        return got, got
    return shifted(message, "section", 1), shifted(message, "section", -1)


def local(probes, jacobian, classes, active, coupling):
    probes, tile = probes[0], jacobian[0]
    count, half = probes.shape[1], probes.shape[0] // 2
    parts = lax.axis_size("cell")
    chunks = MAX_CHUNKS
    while chunks > 1 and count % (8 * chunks * parts):
        chunks -= 1
    rows = count // chunks

    (high, low, message, factors), blocks = first_forward(probes, tile, active, coupling, chunks)
    shared = {"mask": active.astype(jnp.float32), "mask_own": factors[:1]}
    shared["weight"] = class_weight(classes)

    def ready(message):
        below, above = neighbours(message)
        shared.update(first=(message, below, above))
        shared.update(strength=(factors[1:2], factors[2:3] * above[count : count + 1]))
        return message

    def turned(high, low):
        shared["turned"] = turn(high, low)
        return shared["turned"]

    def part(value, chunk):
        return value[chunk * rows : (chunk + 1) * rows]

    def smoothing(here, under, over):
        strength, strength_next = shared["strength"]
        return strength * (here - under) + strength_next * (here - over)

    def hessian(keep, send, smooth):
        sent = yield from sum_cells(keep, send, shared)
        own, other = yield (lambda *values: backward(values, high, low)), *sent
        total, other = yield from sum_data(own, other)
        own = yield (lambda a, b: shared["mask_own"] * (a + b + smooth())), total, other
        return own, swap(own, "dp", 1)

    def second_message(*halves):
        masked = jnp.concatenate(halves, axis=0) * shared["mask_own"]
        shared["second"] = (masked, *neighbours(masked))
        return masked

    def chain(chunk):
        def smooth_first():
            return smoothing(*[part(value, chunk) for value in shared["first"]])

        image = yield from hessian(*blocks[chunk], smooth_first)
        shared[chunk] = image

        def smooth_second():
            return smoothing(*[part(value, chunk) for value in shared["second"]])

        partial = forward_own(image[0], shared["mask"], *shared["turned"])
        sent = yield (lambda *v: forward(*v, shared["mask"], *shared["turned"])), partial, image[1]
        return (yield from hessian(*sent, smooth_second))

    def between():
        yield None
        yield None
        yield None
        yield None
        yield None
        halves = [value for chunk in range(chunks) for value in shared[chunk]]
        return (yield (lambda *values: finish(values)), *halves)

    def after():
        yield ready, message
        yield None
        yield turned, high, low
        yield None
        yield None
        yield second_message, *[shared[chunk][0] for chunk in range(chunks)]

    chains = [(chain(chunk), False) for chunk in range(chunks)]
    chains[1:1] = [(between(), True)]
    halves, first, *rest = in_turn(chains + [(after(), True)], (1, 1, 2, 1, 1))
    for more in rest[:-1]:
        halves = halves + more
    return first[None], finish(halves)[None]


def solution(mesh):
    return jax.shard_map(
        local,
        mesh=mesh,
        in_specs=(
            P("section", "cell", None),
            P("section", "dp", "cell"),
            P("section", "dp"),
            P("section", "cell"),
            P("section", "cell"),
        ),
        out_specs=(P("section", "cell", None), P("section", "cell", None)),
        check_vma=False,
    )
```
